256 devices in a mesh: dp: 8 (over y, core), ctx: 32 (over x, z).
Axes of the slice: x: 4, y: 4, z: 8, core: 2. Of those that a mesh axis runs over, the one named last changes fastest.
Arguments:
- queries: bfloat16 [32768, 2048], P(('dp', 'ctx')), parts along dimension 0, may hold values from -5 to 5
- key_vectors: bfloat16 [32768, 512], P(('dp', 'ctx')), parts along dimension 0, may hold values from -5 to 5
- value_vectors: bfloat16 [32768, 512], P(('dp', 'ctx')), parts along dimension 0, may hold values from -1.5 to 1.5
- output_cotangent: bfloat16 [32768, 2048], P(('dp', 'ctx')), parts along dimension 0, may hold values from -1.5 to 1.5
- doc_lengths: int32 [32], P('dp'), parts along dimension 0, may hold values from 1 to 2176, 4096 in all
- span_of: int32 [256], P('dp'), parts along dimension 0, may hold values from 0 to 31, each once
Outputs:
- attention: bfloat16 [32768, 2048], P(('dp', 'ctx')), parts along dimension 0
- grad_queries: bfloat16 [32768, 2048], P(('dp', 'ctx')), parts along dimension 0
- key_gradient: bfloat16 [32768, 512], P(('dp', 'ctx')), parts along dimension 0
- value_gradient: bfloat16 [32768, 512], P(('dp', 'ctx')), parts along dimension 0
The draws below stay inside these ranges and needn't reach their ends.
There are 8 independent parts, one for each index of `dp`. The reference program is written for one: setup_inputs(seed, part) draws one part's arguments, and reference() takes and returns one part's arrays. A program takes and returns all parts, laid end to end along the dimension named above; each array names one. Nothing has to cross between parts.
Inputs may be any that keep to these rules, and one draw needn't show every extreme that they name: `doc_lengths`: 4 lengths that sum to 4096; the largest is exactly 2176. `span_of`: a permutation of the blocks of the sequence.
All inputs are finite; a program needn't handle non-finite values.
Results may differ from the reference program's by a relative error of at most 0.017.
Values may be sent and summed in bfloat16 or wider, within the bound.
No kernel may reach another device: no remote copies, remote signals or barrier semaphores. Data moves between devices by JAX's collectives and lax.ppermute only.
A program may use at most 128 MiB of HBM per device.

```python
import math
import jax
import jax.numpy as jnp
import numpy as np
from jax import lax

QUERY_HEADS = 16
KEY_VALUE_HEADS = 4
HEAD_SIZE = 128
BLOCK_TOKENS = 128
SEQUENCE_LENGTH = 4096
MAXDOC = 2176
NDOC = 4
N_CTX = 32


def draw_queries(key, part):
    key = jax.random.fold_in(key, 11)
    sampled_draws = jnp.clip(jax.random.normal(key, (SEQUENCE_LENGTH, QUERY_HEADS * HEAD_SIZE), jnp.float32), -5.0, 5.0)
    return sampled_draws.astype(jnp.bfloat16)


def draw_key_vectors(key, part):
    key = jax.random.fold_in(key, 23)
    sampled_draws = jnp.clip(jax.random.normal(key, (SEQUENCE_LENGTH, KEY_VALUE_HEADS * HEAD_SIZE), jnp.float32), -5.0, 5.0)
    return sampled_draws.astype(jnp.bfloat16)


def block_scale(own_key, shape, pieces, smallest, high):
    gain = 1.0
    for position, parts in pieces:
        heights = jax.random.uniform(jax.random.fold_in(jax.random.fold_in(own_key, 6), position), (parts,), jnp.float32, smallest / len(pieces), high / len(pieces))
        gain = gain * jnp.repeat(jnp.exp(heights), shape[position] // parts).reshape((-1,) + (1,) * (len(shape) - 1 - position))
    return gain


def profile(amount, total, reach, slope):
    loads = [(1 << 20) // math.isqrt(grade ** slope) + 1 for grade in range(2, amount + 1)]
    spare, counts = total - reach - (amount - 1), [1] * (amount - 1)
    while spare > 0:
        free = [i for i in range(amount - 1) if counts[i] < reach]
        pool, left = sum([loads[i] for i in free]), spare
        for i in free:
            more = min(reach - counts[i], max(1, left * loads[i] // pool), spare)
            counts[i] = counts[i] + more
            spare = spare - more
    return np.array([reach] + counts)


def ragged(key, amount, total, limit, skew):
    if amount == 2:
        one = jax.random.randint(key, (), max(1, total - limit), min(limit, total - 1) + 1)
        return jnp.stack([one, total - one])
    sizes = jnp.asarray(profile(amount, total, limit, skew), jnp.int32)
    pairs = (amount - 1) // 2
    source_of, receiver = sizes[1:1 + 2 * pairs:2], sizes[2:2 + 2 * pairs:2]
    slack = jnp.minimum(source_of - 1, limit - receiver)
    moved = jax.random.randint(jax.random.fold_in(key, 1), (pairs,), 0, 1 << 20) % (slack + 1)
    sizes = sizes.at[1:1 + 2 * pairs:2].set(source_of - moved).at[2:2 + 2 * pairs:2].set(receiver + moved)
    return sizes[jax.random.permutation(jax.random.fold_in(key, 2), amount)]


def centred(stream_key, dims, deviation, limit, shards=(), held_as=jnp.bfloat16):
    drawn = jax.random.normal(stream_key, dims, jnp.float32) * deviation
    if len(shards) > 0:
        drawn = block_scale(stream_key, dims, shards, -0.22, 0.18) * drawn
    return jnp.clip(drawn, min=-limit, max=limit).astype(held_as)


def setup_inputs(seed: int = 0, part: int = 0) -> dict:
    streams_of = jax.random.split(jax.random.key(seed), 7)
    part_splits = jax.random.split(jax.random.fold_in(streams_of[6], part), 7)
    queries = draw_queries(jax.random.fold_in(jax.random.fold_in(streams_of[6], part), 71), part)
    key_vectors = draw_key_vectors(jax.random.fold_in(jax.random.fold_in(streams_of[6], part), 71), part)
    value_vectors = centred(part_splits[2], (SEQUENCE_LENGTH, KEY_VALUE_HEADS * HEAD_SIZE), 0.25, 1.5, ((0, 32),))
    output_cotangent = centred(part_splits[3], (SEQUENCE_LENGTH, QUERY_HEADS * HEAD_SIZE), 0.25, 1.5, ((0, 32),))
    doc_lengths = ragged(part_splits[4], NDOC, SEQUENCE_LENGTH, MAXDOC, 2).astype(jnp.int32)
    span_of = jax.random.permutation(part_splits[5], N_CTX).astype(jnp.int32)
    return dict(queries=queries, key_vectors=key_vectors, value_vectors=value_vectors, output_cotangent=output_cotangent, doc_lengths=doc_lengths, span_of=span_of)


SCORE_MASK_FILL = -1.0e30


def reference(queries, key_vectors, value_vectors, output_cotangent, doc_lengths, span_of):
    query_groups = QUERY_HEADS // KEY_VALUE_HEADS
    back_spans = MAXDOC // BLOCK_TOKENS
    padding_rows = back_spans * BLOCK_TOKENS
    visible_rows = padding_rows + BLOCK_TOKENS
    inv_root = HEAD_SIZE ** -0.5
    slot_of = jnp.zeros((N_CTX,), jnp.int32).at[span_of].set(jnp.arange(N_CTX, dtype=jnp.int32))

    def natural_layout(array_in):
        return array_in.reshape(N_CTX, BLOCK_TOKENS, -1)[slot_of].reshape(SEQUENCE_LENGTH, -1)

    def placed(array_in):
        return array_in.reshape(N_CTX, BLOCK_TOKENS, -1)[span_of].reshape(SEQUENCE_LENGTH, -1)

    query_natural = natural_layout(queries).astype(jnp.float32)
    output_natural = natural_layout(output_cotangent).astype(jnp.float32)
    padded_keys = jnp.concatenate([jnp.zeros((padding_rows, KEY_VALUE_HEADS * HEAD_SIZE), jnp.float32), natural_layout(key_vectors).astype(jnp.float32)], axis=0)
    padded_values = jnp.concatenate([jnp.zeros((padding_rows, KEY_VALUE_HEADS * HEAD_SIZE), jnp.float32), natural_layout(value_vectors).astype(jnp.float32)], axis=0)
    doc_ends = jnp.cumsum(doc_lengths)
    positions = jnp.arange(SEQUENCE_LENGTH, dtype=jnp.int32)
    doc_ids = jnp.sum((doc_ends[None, :] <= positions[:, None]).astype(jnp.int32), axis=1)
    doc_pad = jnp.concatenate([jnp.full((padding_rows,), -1, jnp.int32), doc_ids], axis=0)

    def one_block(sums, span_id):
        key_gradient_sums, value_gradient_sums = sums
        first_row = (span_id * BLOCK_TOKENS).astype(jnp.int32)
        heads_of_queries = lax.dynamic_slice_in_dim(query_natural, first_row, BLOCK_TOKENS, 0).reshape(BLOCK_TOKENS, KEY_VALUE_HEADS, query_groups, HEAD_SIZE)
        output_heads = lax.dynamic_slice_in_dim(output_natural, first_row, BLOCK_TOKENS, 0).reshape(BLOCK_TOKENS, KEY_VALUE_HEADS, query_groups, HEAD_SIZE)
        heads_of_keys = lax.dynamic_slice_in_dim(padded_keys, first_row, visible_rows, 0).reshape(visible_rows, KEY_VALUE_HEADS, HEAD_SIZE)
        heads_of_values = lax.dynamic_slice_in_dim(padded_values, first_row, visible_rows, 0).reshape(visible_rows, KEY_VALUE_HEADS, HEAD_SIZE)
        query_pos = first_row + jnp.arange(BLOCK_TOKENS, dtype=jnp.int32)
        key_pos = first_row - padding_rows + jnp.arange(visible_rows, dtype=jnp.int32)
        query_doc = lax.dynamic_slice_in_dim(doc_ids, first_row, BLOCK_TOKENS, 0)
        key_doc = lax.dynamic_slice_in_dim(doc_pad, first_row, visible_rows, 0)
        allowed = (key_doc[None, :] == query_doc[:, None]) & (key_pos[None, :] <= query_pos[:, None])
        scores = jnp.where(allowed, jnp.einsum("qghd,rgd->ghqr", heads_of_queries, heads_of_keys) * inv_root, SCORE_MASK_FILL)
        row_max = jnp.max(scores, axis=-1)
        row_total = jnp.sum(jnp.where(allowed, jnp.exp(scores - row_max[..., None]), 0.0), axis=-1)
        log_totals = row_max + jnp.log(row_total)
        exact_weights = jnp.where(allowed, jnp.exp(scores - log_totals[..., None]), 0.0)
        weights = exact_weights.astype(jnp.bfloat16).astype(jnp.float32)
        attention = jnp.einsum("ghqr,rgd->qghd", weights, heads_of_values).astype(jnp.bfloat16)
        out_dot = jnp.transpose(jnp.sum(attention.astype(jnp.float32) * output_heads, axis=-1), (1, 2, 0))
        grad_weights = jnp.einsum("qghd,rgd->ghqr", output_heads, heads_of_values)
        grad_scores = (exact_weights * (grad_weights - out_dot[..., None])).astype(jnp.bfloat16).astype(jnp.float32)
        grad_query = (inv_root * jnp.einsum("ghqr,rgd->qghd", grad_scores, heads_of_keys)).astype(jnp.bfloat16)
        key_portion = (inv_root * jnp.einsum("ghqr,qghd->rgd", grad_scores, heads_of_queries)).astype(jnp.bfloat16)
        value_portion = jnp.einsum("ghqr,qghd->rgd", weights, output_heads).astype(jnp.bfloat16)
        current_key = lax.dynamic_slice_in_dim(key_gradient_sums, first_row, visible_rows, 0)
        current_value = lax.dynamic_slice_in_dim(value_gradient_sums, first_row, visible_rows, 0)
        key_gradient_sums = lax.dynamic_update_slice_in_dim(key_gradient_sums, current_key + key_portion.reshape(visible_rows, KEY_VALUE_HEADS * HEAD_SIZE).astype(jnp.float32), first_row, 0)
        value_gradient_sums = lax.dynamic_update_slice_in_dim(value_gradient_sums, current_value + value_portion.reshape(visible_rows, KEY_VALUE_HEADS * HEAD_SIZE).astype(jnp.float32), first_row, 0)
        return (key_gradient_sums, value_gradient_sums), (attention.reshape(BLOCK_TOKENS, QUERY_HEADS * HEAD_SIZE), grad_query.reshape(BLOCK_TOKENS, QUERY_HEADS * HEAD_SIZE))

    initial_sums = (jnp.zeros((padding_rows + SEQUENCE_LENGTH, KEY_VALUE_HEADS * HEAD_SIZE), jnp.float32), jnp.zeros((padding_rows + SEQUENCE_LENGTH, KEY_VALUE_HEADS * HEAD_SIZE), jnp.float32))
    (key_gradient_sums, value_gradient_sums), (attention, grad_queries) = lax.scan(one_block, initial_sums, jnp.arange(N_CTX, dtype=jnp.int32))
    key_gradient = key_gradient_sums[padding_rows:].astype(jnp.bfloat16)
    value_gradient = value_gradient_sums[padding_rows:].astype(jnp.bfloat16)
    return (placed(attention.reshape(SEQUENCE_LENGTH, QUERY_HEADS * HEAD_SIZE)), placed(grad_queries.reshape(SEQUENCE_LENGTH, QUERY_HEADS * HEAD_SIZE)), placed(key_gradient), placed(value_gradient))
```

```python
import functools

import jax
import jax.numpy as jnp
from jax import lax
from jax.experimental import pallas as pl
from jax.experimental.pallas import tpu as pltpu
from jax.sharding import Mesh, PartitionSpec as P

HEADS = 4
D = 128
B = 128
NX, NZ = 4, 8
NB = NX * NZ
W = HEADS * B
CHUNKS = 9
SCALE = D ** -0.5
SCALE_LOG2 = SCALE * 1.4426950408889634
FILL = -1e30
BF, F32 = jnp.bfloat16, jnp.float32


def nt(a, b):
    return lax.dot_general(a, b, (((1,), (1,)), ((), ())), preferred_element_type=F32)


def tn(a, b):
    return lax.dot_general(a, b, (((0,), (0,)), ((), ())), preferred_element_type=F32)


def nn(a, b):
    return lax.dot_general(a, b, (((1,), (0,)), ((), ())), preferred_element_type=F32)


def attention_kernel(span_ref, doc_ref, z_ref, q_ref, do_ref, kv_ref,
                     o_ref, dq_ref, dkv_ref, p_ref, acc_ref, slot_ref, pb_ref):
    z = z_ref[0]
    ends = []
    total = jnp.int32(0)
    for i in range(4):
        total = total + doc_ref[i]
        ends.append(total)

    def place(i, carry):
        slot_ref[span_ref[i]] = lax.rem(i, NZ) * NX + i // NZ
        return carry

    lax.fori_loop(0, NB, place, 0)
    slot_ref[NB] = 0
    acc_ref[...] = jnp.zeros_like(acc_ref)

    def stacked(ref, i):
        rows = ref[i]
        return jnp.concatenate([rows[:, h * D:(h + 1) * D] for h in range(HEADS)], axis=0)

    def one_block(i, carry):
        span = span_ref[i * NZ + z]
        first = span * B
        start_first = jnp.int32(0)
        lane = lax.broadcasted_iota(jnp.int32, (1, W), 1)
        q_pos = first + lax.rem(lane, B)
        q_start = jnp.zeros((1, W), jnp.int32)
        start_last = jnp.int32(0)
        for e in ends:
            start_first = jnp.where(e <= first, e, start_first)
            start_last = jnp.where(e <= first + B - 1, e, start_last)
            q_start = jnp.where(e <= q_pos, e, q_start)
        low = start_first // B
        count = (span - low) // 2 + 1
        qs = stacked(q_ref, i)

        def pair(c):
            s = low + 2 * c
            return s, slot_ref[s], slot_ref[s + 1]

        def keys(a, b):
            return jnp.concatenate([kv_ref[a, :, :D], kv_ref[b, :, :D]], axis=0)

        def values(a, b):
            return jnp.concatenate([kv_ref[a, :, D:], kv_ref[b, :, D:]], axis=0)

        def score_step(c, m):
            s, a, b = pair(c)
            st = nt(keys(a, b), qs) * SCALE_LOG2
            k_pos = s * B + lax.broadcasted_iota(jnp.int32, (2 * B, W), 0)
            st = jnp.where((k_pos >= q_start) & (k_pos <= q_pos), st, FILL)
            p_ref[c] = st
            return jnp.maximum(m, jnp.max(st, axis=0, keepdims=True))

        m = lax.fori_loop(0, count, score_step, jnp.full((1, W), FILL, F32))

        def weigh_step(c, state):
            l, ot = state
            s, a, b = pair(c)
            p = jnp.exp2(p_ref[c] - m)
            pb = p.astype(BF)
            pb_ref[c] = pb
            return l + jnp.sum(p, axis=0, keepdims=True), ot + tn(values(a, b), pb)

        l, ot = lax.fori_loop(
            0, count, weigh_step, (jnp.zeros((1, W), F32), jnp.zeros((D, W), F32))
        )
        inv = 1.0 / l
        ob = (ot * inv).astype(BF)
        dos = stacked(do_ref, i)
        dot = jnp.concatenate(
            [dos[h * B:(h + 1) * B, :].astype(F32).T for h in range(HEADS)], axis=1
        )
        dotn = dot * inv
        dos = jnp.concatenate(
            [dotn[:, h * B:(h + 1) * B].T for h in range(HEADS)], axis=0
        ).astype(BF)
        delta = jnp.sum(ob.astype(F32) * dotn, axis=0, keepdims=True)

        def back_step(c, dqt):
            s, a, b = pair(c)
            pb = pb_ref[c]
            dp = nt(values(a, b), dos)
            ds = (pb.astype(F32) * (dp - delta)).astype(BF)
            dv = nn(pb, dos)
            dk = nn(ds, qs)
            acc_ref[a, :, :D] += dk[:B]
            acc_ref[b, :, :D] += dk[B:]
            acc_ref[a, :, D:] += dv[:B]
            acc_ref[b, :, D:] += dv[B:]
            return dqt + tn(keys(a, b), ds)

        dqt = lax.fori_loop(0, count, back_step, jnp.zeros((D, W), F32))
        for h in range(HEADS):
            cols = slice(h * B, (h + 1) * B)
            o_ref[i, :, cols] = ob[:, cols].astype(F32).T.astype(BF)
            dq_ref[i, :, cols] = (dqt[:, cols] * SCALE).T.astype(BF)
        return carry

    lax.fori_loop(0, NX, one_block, 0)

    def put(i, carry):
        dkv_ref[i, :, :D] = (acc_ref[i, :, :D] * SCALE).astype(BF)
        dkv_ref[i, :, D:] = acc_ref[i, :, D:].astype(BF)
        return carry

    lax.fori_loop(0, NB, put, 0)


def attend(span_of, doc_lengths, z, q, do, kv):
    vm = pl.BlockSpec(memory_space=pltpu.VMEM)
    sm = pl.BlockSpec(memory_space=pltpu.SMEM)
    return pl.pallas_call(
        attention_kernel,
        in_specs=[sm, sm, sm, vm, vm, vm],
        out_specs=[vm, vm, vm],
        out_shape=[
            jax.ShapeDtypeStruct((NX, B, W), BF),
            jax.ShapeDtypeStruct((NX, B, W), BF),
            jax.ShapeDtypeStruct((NB, B, 2 * D), BF),
        ],
        scratch_shapes=[
            pltpu.VMEM((CHUNKS, 2 * B, W), F32),
            pltpu.VMEM((NB, B, 2 * D), F32),
            pltpu.SMEM((NB + 8,), jnp.int32),
            pltpu.VMEM((CHUNKS, 2 * B, W), BF),
        ],
        compiler_params=pltpu.CompilerParams(vmem_limit_bytes=48 * 2 ** 20),
        name="attention",
    )(span_of, doc_lengths, z, q, do, kv)


def on_device(queries, key_vectors, value_vectors, output_cotangent, doc_lengths, span_of):
    z = lax.axis_index("z").astype(jnp.int32).reshape(1)
    k = key_vectors.reshape(B, NX, D)
    v = value_vectors.reshape(B, NX, D)
    kv = jnp.concatenate([k, v], axis=2).transpose(1, 0, 2)
    kv = lax.all_to_all(kv, "x", 0, 0)
    kv = lax.all_gather(kv, "z", axis=0, tiled=True)
    q = lax.all_to_all(queries.reshape(B, NX, W).transpose(1, 0, 2), "x", 0, 0)
    do = lax.all_to_all(output_cotangent.reshape(B, NX, W).transpose(1, 0, 2), "x", 0, 0)
    o, dq, dkv = attend(span_of, doc_lengths, z, q, do, kv)
    dkv = lax.psum_scatter(dkv, "z", scatter_dimension=0, tiled=True)
    dkv = lax.all_to_all(dkv, "x", 0, 0)
    o = lax.all_to_all(o, "x", 0, 0).transpose(1, 0, 2).reshape(B, NX * W)
    dq = lax.all_to_all(dq, "x", 0, 0).transpose(1, 0, 2).reshape(B, NX * W)
    dkv = dkv.transpose(1, 0, 2)
    dk = dkv[:, :, :D].reshape(B, NX * D)
    dv = dkv[:, :, D:].reshape(B, NX * D)
    return o, dq, dk, dv


def solution(mesh):
    split = Mesh(mesh.devices.reshape(-1, NX, NZ), ("dp", "x", "z"))
    rows = P(("dp", "x", "z"), None)
    part = P("dp")
    return jax.shard_map(
        on_device,
        mesh=split,
        in_specs=(rows, rows, rows, rows, part, part),
        out_specs=(rows, rows, rows, rows),
        check_vma=False,
    )
```

```python
import functools

import jax
import jax.numpy as jnp
from jax import lax
from jax.experimental import pallas as pl
from jax.experimental.pallas import tpu as pltpu
from jax.sharding import Mesh, PartitionSpec as P

HEADS = 4
D = 128
B = 128
NX, NH, NL = 4, 4, 2
W = HEADS * B
SEEN = 18
STEP = 4
STEPS = -(-SEEN // STEP)
SCALE = D ** -0.5
SCALE_LOG2 = SCALE * 1.4426950408889634
FILL = -1e30
BF, F32 = jnp.bfloat16, jnp.float32
VM = pl.BlockSpec(memory_space=pltpu.VMEM)
SM = pl.BlockSpec(memory_space=pltpu.SMEM)
ROOM = pltpu.CompilerParams(vmem_limit_bytes=48 * 2 ** 20)


def nt(a, b):
    return lax.dot_general(a, b, (((1,), (1,)), ((), ())), preferred_element_type=F32)


def tn(a, b):
    return lax.dot_general(a, b, (((0,), (0,)), ((), ())), preferred_element_type=F32)


def nn(a, b):
    return lax.dot_general(a, b, (((1,), (0,)), ((), ())), preferred_element_type=F32)


def sds(*shape, dtype=BF):
    return jax.ShapeDtypeStruct(shape, dtype)


class Places:
    def __init__(self, fact_ref, me_ref, shifts, table_ref, list_ref):
        self.fact_ref, self.me_ref = fact_ref, me_ref
        self.table_ref, self.list_ref = table_ref, list_ref
        self.count = 2 * NH * len(shifts)
        self.ends = []
        total = jnp.int32(0)
        for i in range(4):
            total = total + fact_ref[NX * NH * NL + i]
            self.ends.append(total)
        for side in range(2):
            for k, dx in enumerate(shifts):
                for step in range(NH):
                    index = (side * len(shifts) + k) * NH + step
                    table_ref[index] = self.span(dx, step, side)

    def span(self, dx, step, side):
        e, x, zh = self.me_ref[0], self.me_ref[1], self.me_ref[2]
        from_x = lax.rem(x + NX - dx, NX)
        from_zh = lax.rem(zh + NH - step, NH)
        return self.fact_ref[(from_x * NH + from_zh) * NL + lax.rem(e + side, NL)]

    def of_query_block(self, i):
        span = self.span(0, i, 0)
        first = span * B
        self.q_pos = first + lax.rem(lax.broadcasted_iota(jnp.int32, (1, W), 1), B)
        self.q_start = jnp.zeros((1, W), jnp.int32)
        start_first = jnp.int32(0)
        for e in self.ends:
            start_first = jnp.where(e <= first, e, start_first)
            self.q_start = jnp.where(e <= self.q_pos, e, self.q_start)
        low = start_first // B
        n = jnp.int32(0)
        for j in range(self.count):
            s = self.table_ref[j]
            self.list_ref[n] = j
            n = n + jnp.where((s >= low) & (s <= span), 1, 0)
        for j in range(STEP - 1):
            self.list_ref[n + j] = 0
        self.n = n
        return (n + STEP - 1) // STEP

    def blocks(self, c):
        return [self.list_ref[STEP * c + j] for j in range(STEP)]

    def mask(self, c, blocks):
        row = lax.broadcasted_iota(jnp.int32, (B, W), 0)
        parts = []
        for j, block in enumerate(blocks):
            first = jnp.where(STEP * c + j < self.n, self.table_ref[block] * B, SEEN * B * 4)
            k_pos = row + first
            parts.append((k_pos >= self.q_start) & (k_pos <= self.q_pos))
        return jnp.concatenate(parts, axis=0)


def stacked(ref, i):
    return jnp.concatenate([ref[i, :, h * D:(h + 1) * D] for h in range(HEADS)], axis=0)


def taken(ref, blocks, cols):
    return jnp.concatenate([ref[block, :, cols] for block in blocks], axis=0)


SHIFTS = (0, 1, 2, 3)
KEYS, VALUES = slice(0, D), slice(D, 2 * D)


def forward_kernel(fact_ref, me_ref, q_ref, do_ref, own_ref, sib_ref, o_ref, stat_ref,
                   s_ref, kv_ref, table_ref, list_ref):
    half = NX * NH
    kv_ref[:half] = own_ref[...]
    kv_ref[half:] = sib_ref[...]
    places = Places(fact_ref, me_ref, SHIFTS, table_ref, list_ref)

    def one_block(i, carry):
        steps = places.of_query_block(i)
        qs = stacked(q_ref, i)

        def score_step(c, m):
            blocks = places.blocks(c)
            st = nt(taken(kv_ref, blocks, KEYS), qs) * SCALE_LOG2
            st = jnp.where(places.mask(c, blocks), st, FILL)
            s_ref[c] = st
            return jnp.maximum(m, jnp.max(st.reshape(-1, 8, W), axis=0))

        m = lax.fori_loop(0, steps, score_step, jnp.full((8, W), FILL, F32))
        m = jnp.max(m, axis=0, keepdims=True)

        def weigh_step(c, state):
            l, ot = state
            blocks = places.blocks(c)
            p = jnp.exp2(s_ref[c] - m)
            return (
                l + jnp.sum(p.reshape(-1, 8, W), axis=0),
                ot + tn(taken(kv_ref, blocks, VALUES), p.astype(BF)),
            )

        state = jnp.zeros((8, W), F32), jnp.zeros((D, W), F32)
        l, ot = lax.fori_loop(0, steps, weigh_step, state)
        l = jnp.sum(l, axis=0, keepdims=True)
        ob = (ot * (1.0 / l)).astype(BF)
        delta = []
        for h in range(HEADS):
            cols = slice(h * B, (h + 1) * B)
            of = ob[:, cols].astype(F32)
            o_ref[i, :, cols] = of.T.astype(BF)
            dot = do_ref[i, :, cols].astype(F32).T
            delta.append(jnp.sum(of * dot, axis=0, keepdims=True))
        stat_ref[i, 0:1, :] = m + jnp.log2(l)
        stat_ref[i, 1:2, :] = jnp.concatenate(delta, axis=1)
        return carry

    lax.fori_loop(0, NH, one_block, 0)


def forward(facts, me, q, do, own, sib):
    blocks = 2 * NX * NH
    return pl.pallas_call(
        forward_kernel,
        in_specs=[SM] * 2 + [VM] * 4,
        out_specs=[VM] * 2,
        out_shape=[sds(NH, B, W), sds(NH, 8, W, dtype=F32)],
        scratch_shapes=[
            pltpu.VMEM((STEPS, STEP * B, W), F32),
            pltpu.VMEM((blocks, B, 2 * D), BF),
            pltpu.SMEM((blocks,), jnp.int32),
            pltpu.SMEM((blocks + 8,), jnp.int32),
        ],
        compiler_params=ROOM,
        cost_estimate=pl.CostEstimate(flops=8 * 10 ** 9, bytes_accessed=4 * 10 ** 6, transcendentals=0),
        name="forward",
    )(facts, me, q, do, own, sib)


def backward_kernel(shifts, first, last, *refs):
    refs = list(refs)
    n = len(shifts)
    fact_ref, me_ref, q_ref, do_ref, stat_ref = refs[:5]
    chunks, rest = refs[5:5 + 2 * n], refs[5 + 2 * n:]
    if not first:
        dqt_in = rest[0]
        rest = rest[1:]
    if last:
        o_ref = rest[0]
        rest = rest[1:]
    own_out, sib_out, dq_out, s_ref, acc_ref, kv_ref, table_ref, list_ref = rest
    for k, ref in enumerate(chunks):
        kv_ref[k * NH:(k + 1) * NH] = ref[...]
    places = Places(fact_ref, me_ref, shifts, table_ref, list_ref)
    acc_ref[...] = jnp.zeros_like(acc_ref)

    def one_block(i, carry):
        steps = places.of_query_block(i)
        qs, dos = stacked(q_ref, i), stacked(do_ref, i)
        lse, delta = stat_ref[i, 0:1, :], stat_ref[i, 1:2, :]

        def step(c, dqt):
            blocks = places.blocks(c)
            keys = taken(kv_ref, blocks, KEYS)
            st = nt(keys, qs) * SCALE_LOG2 - lse
            p = jnp.exp2(jnp.where(places.mask(c, blocks), st, FILL))
            dp = nt(taken(kv_ref, blocks, VALUES), dos)
            ds = (p * (dp - delta)).astype(BF)
            dv = nn(p.astype(BF), dos)
            dk = nn(ds, qs)
            for j, block in enumerate(blocks):
                acc_ref[block, :, KEYS] += dk[j * B:(j + 1) * B]
                acc_ref[block, :, VALUES] += dv[j * B:(j + 1) * B]
            return dqt + tn(keys, ds)

        dqt = lax.fori_loop(0, steps, step, jnp.zeros((D, W), F32) if first else dqt_in[i])
        if last:
            dq_out[i, :, :W] = o_ref[i]
            for h in range(HEADS):
                cols = slice(h * B, (h + 1) * B)
                dq_out[i, :, W + h * B:W + (h + 1) * B] = (dqt[:, cols] * SCALE).T.astype(BF)
        else:
            dq_out[i] = dqt
        return carry

    lax.fori_loop(0, NH, one_block, 0)
    for side, ref in enumerate((own_out, sib_out)):
        for j in range(n * NH):
            at = side * n * NH + j
            ref[j, :, KEYS] = (acc_ref[at, :, KEYS] * SCALE).astype(BF)
            ref[j, :, VALUES] = acc_ref[at, :, VALUES].astype(BF)


def backward(shifts, facts, me, q, do, stat, own, sib, dqt, o):
    first, last = dqt is None, o is not None
    n = len(shifts)
    tail = ([] if first else [dqt]) + ([o] if last else [])
    args = [facts, me, q, do, stat] + [own] * n + [sib] * n + tail
    chunk_specs = [
        pl.BlockSpec((NH, B, 2 * D), lambda g, k=SHIFTS.index(dx): (k, 0, 0)) for dx in shifts
    ]
    dq = sds(NH, B, 2 * W) if last else sds(NH, D, W, dtype=F32)
    return pl.pallas_call(
        functools.partial(backward_kernel, shifts, first, last),
        grid=(1,),
        in_specs=[SM] * 2 + [VM] * 3 + chunk_specs * 2 + [VM] * len(tail),
        out_specs=[VM] * 3,
        out_shape=[sds(n * NH, B, 2 * D)] * 2 + [dq],
        scratch_shapes=[
            pltpu.VMEM((STEP * B, W), F32),
            pltpu.VMEM((2 * n * NH, B, 2 * D), F32),
            pltpu.VMEM((2 * n * NH, B, 2 * D), BF),
            pltpu.SMEM((2 * n * NH,), jnp.int32),
            pltpu.SMEM((2 * n * NH + 8,), jnp.int32),
        ],
        compiler_params=ROOM,
        cost_estimate=pl.CostEstimate(
            flops=5 * n * 10 ** 9, bytes_accessed=4 * 10 ** 6, transcendentals=0
        ),
        name="backward",
    )(*args)


def pack_kernel(me_ref, *refs):
    arrays, outs = refs[:-NH], refs[-NH:]
    for s, out in enumerate(outs):
        group, at = lax.rem(me_ref[2] + s, NH), 0
        for ref in arrays:
            width = ref.shape[1] // NH
            out[:, at:at + width] = ref[:, pl.ds(pl.multiple_of(group * width, width), width)]
            at += width


def pack(me, *arrays):
    width = sum(a.shape[1] for a in arrays) // NH
    return pl.pallas_call(
        pack_kernel,
        in_specs=[SM] + [VM] * len(arrays),
        out_specs=[VM] * NH,
        out_shape=[sds(B, width)] * NH,
        name="pack",
    )(me, *arrays)


def unpack_kernel(me_ref, *refs):
    odq, dkv, outs = refs[:NH], refs[NH:2 * NH], refs[2 * NH:]
    for s in range(NH):
        group = lax.rem(me_ref[2] + s, NH)
        for piece, pair in ((odq[s], outs[:2]), (dkv[s], outs[2:])):
            width = piece.shape[1] // 2
            cols = pl.ds(pl.multiple_of(group * width, width), width)
            for k, out in enumerate(pair):
                out[:, cols] = piece[:, k * width:(k + 1) * width]


def unpack(me, odq, dkv):
    return pl.pallas_call(
        unpack_kernel,
        in_specs=[SM] + [VM] * (2 * NH),
        out_specs=[VM] * 4,
        out_shape=[sds(B, NH * W)] * 2 + [sds(B, NH * D)] * 2,
        name="unpack",
    )(me, *odq, *dkv)


def by_heads(pieces, sign):
    out = []
    for s in range(NH):
        perm = [
            ((c * NH + h) * NL + l, (l * NH + (h + sign * s) % NH) * NL + c)
            for c in range(2) for h in range(NH) for l in range(NL)
        ]
        out.append(lax.ppermute(pieces[s], ("core", "zh", "zl"), perm))
    return out


def to_x(array, shift):
    return lax.ppermute(array, "x", [(i, (i + shift) % NX) for i in range(NX)])


def to_sibling(array):
    return lax.ppermute(array, "core", [(0, 1), (1, 0)])


def on_device(queries, key_vectors, value_vectors, output_cotangent, doc_lengths, span_of):
    core, zl = lax.axis_index("core"), lax.axis_index("zl")
    me = jnp.stack([core, lax.axis_index("x"), lax.axis_index("zh")]).astype(jnp.int32)
    kvq = jnp.stack(by_heads(pack(me, key_vectors, value_vectors, queries), 1))
    kv, q = kvq[:, :, :2 * D], kvq[:, :, 2 * D:]
    do_pieces = pack(me, output_cotangent)
    do = jnp.stack(by_heads(do_pieces, 1))
    facts = jnp.concatenate([span_of, doc_lengths])
    facts = jnp.where(core == zl, facts, to_sibling(facts))
    own = jnp.concatenate([kv] + [to_x(kv, dx) for dx in SHIFTS[1:]])
    own, do, facts = lax.optimization_barrier((own, do, facts))
    sib = to_sibling(own)
    o, stat = forward(facts, me, q, do, own, sib)
    args = facts, me, q, do, stat, own, sib
    mine2, theirs2, dqt = backward((2,), *args, None, None)
    mine13, theirs13, dqt = backward((1, 3), *args, dqt, None)
    mine0, theirs0, odq = backward((0,), *args, dqt, o)

    def added(mine, theirs):
        return mine.astype(F32) + to_sibling(theirs).astype(F32)

    sum2, sum13 = added(mine2, theirs2).astype(BF), added(mine13, theirs13).astype(BF)
    total = added(mine0, theirs0)
    for array, dx in ((sum2, 2), (sum13[:NH], 1), (sum13[NH:], 3)):
        total = total + to_x(array, -dx).astype(F32)
    total = total.astype(BF)
    dkv = by_heads([total[s] for s in range(NH)], -1)
    odq = by_heads([odq[s] for s in range(NH)], -1)
    return unpack(me, odq, dkv)


def solution(mesh):
    split = Mesh(
        mesh.devices.reshape(-1, 2, NX, NH, NL), ("y", "core", "x", "zh", "zl")
    )
    rows = P(("y", "core", "x", "zh", "zl"), None)
    part = P(("y", "core"))
    return jax.shard_map(
        on_device,
        mesh=split,
        in_specs=(rows, rows, rows, rows, part, part),
        out_specs=(rows, rows, rows, rows),
        check_vma=False,
    )
```

```python
import jax
import jax.numpy as jnp
from jax import lax
from jax.experimental import pallas as pl
from jax.experimental.pallas import tpu as pltpu
from jax.sharding import Mesh, PartitionSpec as P

HEADS = 4
D = 128
B = 128
NX, NH, NL = 4, 4, 2
HEAD_AXIS, SEQ_AXIS = "zh", "x"
W = HEADS * B
SEEN = 18
STEP = 4
STEPS = (SEEN + 1 + STEP - 1) // STEP
SCALE = D ** -0.5
SCALE_LOG2 = SCALE * 1.4426950408889634
FILL = -1e30
BF, F32 = jnp.bfloat16, jnp.float32
VM = pl.BlockSpec(memory_space=pltpu.VMEM)
SM = pl.BlockSpec(memory_space=pltpu.SMEM)
ROOM = pltpu.CompilerParams(vmem_limit_bytes=48 * 2 ** 20)


def nt(a, b):
    return lax.dot_general(a, b, (((1,), (1,)), ((), ())), preferred_element_type=F32)


def tn(a, b):
    return lax.dot_general(a, b, (((0,), (0,)), ((), ())), preferred_element_type=F32)


def nn(a, b):
    return lax.dot_general(a, b, (((1,), (0,)), ((), ())), preferred_element_type=F32)


def sds(*shape, dtype=BF):
    return jax.ShapeDtypeStruct(shape, dtype)


class Places:
    def __init__(self, fact_ref, me_ref, shifts, table_ref, list_ref):
        self.fact_ref, self.me_ref = fact_ref, me_ref
        self.table_ref, self.list_ref = table_ref, list_ref
        self.count = 2 * NH * len(shifts)
        self.ends = []
        total = jnp.int32(0)
        for i in range(4):
            total = total + fact_ref[NX * NH * NL + i]
            self.ends.append(total)
        for k, dx in enumerate(shifts):
            for side in range(2):
                for step in range(NH):
                    table_ref[(k * 2 + side) * NH + step] = self.span(dx, step, side)

    def span(self, dx, step, side):
        e, seq, head = self.me_ref[0], self.me_ref[1], self.me_ref[2]
        from_x = lax.rem(seq + NX - dx, NX)
        from_zh = lax.rem(head + NH - step, NH)
        return self.fact_ref[(from_x * NH + from_zh) * NL + lax.rem(e + side, NL)]

    def of_query_block(self, i):
        span = self.span(0, i, 0)
        first = span * B
        self.q_pos = first + lax.rem(lax.broadcasted_iota(jnp.int32, (1, W), 1), B)
        self.q_start = jnp.zeros((1, W), jnp.int32)
        start_first = jnp.int32(0)
        for e in self.ends:
            start_first = jnp.where(e <= first, e, start_first)
            self.q_start = jnp.where(e <= self.q_pos, e, self.q_start)
        self.low, self.high = start_first // B, span

    def listed(self, n, entries):
        for j in entries:
            s = self.table_ref[j]
            self.list_ref[0, n] = j
            self.list_ref[1, n] = s * B
            n = n + jnp.where((s >= self.low) & (s <= self.high), 1, 0)
        return n

    def padded(self, n):
        for j in range(STEP):
            self.list_ref[0, n + j] = 0
            self.list_ref[1, n + j] = SEEN * B * 4

    def blocks(self, at, number):
        return [self.list_ref[0, at + j] for j in range(number)]

    def mask(self, at, number):
        row = lax.broadcasted_iota(jnp.int32, (B, W), 0)
        parts = []
        for j in range(number):
            k_pos = row + self.list_ref[1, at + j]
            parts.append((k_pos >= self.q_start) & (k_pos <= self.q_pos))
        return jnp.concatenate(parts, axis=0)


def stacked(ref, i, which):
    return jnp.concatenate(
        [ref[i, :, (which * HEADS + h) * D:(which * HEADS + h + 1) * D] for h in range(HEADS)], axis=0
    )


def taken(ref, blocks, cols):
    return jnp.concatenate([ref[block, :, cols] for block in blocks], axis=0)


SHIFTS = (1, 2, 3, 0)
EARLY = (2,)
FAR = 2 * NH * (NX - 1)
KEYS, VALUES = slice(0, D), slice(D, 2 * D)


def gradients(dqt, keys, p, dp, delta, qs, dos, acc_ref, blocks):
    ds = (p * (dp - delta)).astype(BF)
    dv = nn(p.astype(BF), dos)
    dk = nn(ds, qs)
    for j, block in enumerate(blocks):
        acc_ref[block, :, KEYS] += dk[j * B:(j + 1) * B]
        acc_ref[block, :, VALUES] += dv[j * B:(j + 1) * B]
    return dqt + tn(keys, ds)


def put_gradients(own_out, sib_out, acc_ref):
    for ref, side in ((own_out, 0), (sib_out, 1)):
        for j in range(ref.shape[0]):
            at = (j // NH * 2 + side) * NH + j % NH
            ref[j, :, KEYS] = (acc_ref[at, :, KEYS] * SCALE).astype(BF)
            ref[j, :, VALUES] = acc_ref[at, :, VALUES].astype(BF)


def far_kernel(fact_ref, me_ref, qdo_ref, own_ref, sib_ref,
               o_ref, stat_ref, own_out, sib_out, dqt_out,
               s_ref, kv_ref, acc_ref, table_ref, list_ref):
    for k, dx in enumerate(SHIFTS):
        kv_ref[2 * k * NH:(2 * k + 1) * NH] = own_ref[dx * NH:(dx + 1) * NH]
        kv_ref[(2 * k + 1) * NH:(2 * k + 2) * NH] = sib_ref[dx * NH:(dx + 1) * NH]
    places = Places(fact_ref, me_ref, SHIFTS, table_ref, list_ref)
    acc_ref[...] = jnp.zeros_like(acc_ref)

    def one_block(i, carry):
        places.of_query_block(i)
        far = places.listed(jnp.int32(0), range(FAR))
        list_ref[0, far] = 0
        list_ref[1, far] = SEEN * B * 4
        far = (far + 1) // 2 * 2
        n = places.listed(far, range(FAR, 2 * NX * NH))
        places.padded(n)
        steps = (n + STEP - 1) // STEP
        qs, dos = stacked(qdo_ref, i, 0), stacked(qdo_ref, i, 1)

        def score_step(c, m):
            blocks = places.blocks(STEP * c, STEP)
            st = nt(taken(kv_ref, blocks, KEYS), qs) * SCALE_LOG2
            st = jnp.where(places.mask(STEP * c, STEP), st, FILL)
            s_ref[c] = st
            return jnp.maximum(m, jnp.max(st.reshape(-1, 8, W), axis=0))

        m = lax.fori_loop(0, steps, score_step, jnp.full((8, W), FILL, F32))
        m = jnp.max(m, axis=0, keepdims=True)

        def weigh_step(c, state):
            l, ot = state
            blocks = places.blocks(STEP * c, STEP)
            p = jnp.exp2(s_ref[c] - m)
            return (
                l + jnp.sum(p.reshape(-1, 8, W), axis=0),
                ot + tn(taken(kv_ref, blocks, VALUES), p.astype(BF)),
            )

        state = jnp.zeros((8, W), F32), jnp.zeros((D, W), F32)
        l, ot = lax.fori_loop(0, steps, weigh_step, state)
        l = jnp.sum(l, axis=0, keepdims=True)
        ob = (ot * (1.0 / l)).astype(BF)
        delta = []
        for h in range(HEADS):
            cols = slice(h * B, (h + 1) * B)
            of = ob[:, cols].astype(F32)
            o_ref[i, :, cols] = of.T.astype(BF)
            dot = qdo_ref[i, :, W + h * B:W + (h + 1) * B].astype(F32).T
            delta.append(jnp.sum(of * dot, axis=0, keepdims=True))
        delta = jnp.concatenate(delta, axis=1)
        lse = m + jnp.log2(l)
        stat_ref[i, 0:1, :] = lse
        stat_ref[i, 1:2, :] = delta

        def back_step(c, part, number, dqt):
            at = STEP * c + part
            blocks = places.blocks(at, number)
            p = jnp.exp2(s_ref[c, part * B:(part + number) * B] - lse)
            dp = nt(taken(kv_ref, blocks, VALUES), dos)
            keys = taken(kv_ref, blocks, KEYS)
            return gradients(dqt, keys, p, dp, delta, qs, dos, acc_ref, blocks)

        wide = far // STEP
        dqt = lax.fori_loop(
            0, wide, lambda c, t: back_step(c, 0, STEP, t), jnp.zeros((D, W), F32)
        )
        dqt_out[i] = lax.fori_loop(
            wide, (far + STEP - 1) // STEP, lambda c, t: back_step(c, 0, STEP // 2, t), dqt
        )
        return carry

    lax.fori_loop(0, NH, one_block, 0)
    put_gradients(own_out, sib_out, acc_ref)


def far(facts, me, qdo, own, sib):
    blocks = 2 * NX * NH
    return pl.pallas_call(
        far_kernel,
        in_specs=[SM] * 2 + [VM] * 3,
        out_specs=[VM] * 5,
        out_shape=[sds(NH, B, W), sds(NH, 8, W, dtype=F32)]
        + [sds(FAR // 2, B, 2 * D)] * 2 + [sds(NH, D, W, dtype=F32)],
        scratch_shapes=[
            pltpu.VMEM((STEPS, STEP * B, W), F32),
            pltpu.VMEM((blocks, B, 2 * D), BF),
            pltpu.VMEM((FAR, B, 2 * D), F32),
            pltpu.SMEM((blocks,), jnp.int32),
            pltpu.SMEM((2, blocks + 8), jnp.int32),
        ],
        compiler_params=ROOM,
        cost_estimate=pl.CostEstimate(flops=20 * 10 ** 9, bytes_accessed=4 * 10 ** 6, transcendentals=0),
        name="far",
    )(facts, me, qdo, own, sib)


def near_kernel(fact_ref, me_ref, qdo_ref, stat_ref, own_ref, sib_ref, dqt_ref,
                own_out, sib_out, dq_ref, kv_ref, acc_ref, table_ref, list_ref):
    kv_ref[:NH] = own_ref[...]
    kv_ref[NH:] = sib_ref[...]
    places = Places(fact_ref, me_ref, (0,), table_ref, list_ref)
    acc_ref[...] = jnp.zeros_like(acc_ref)

    def one_block(i, carry):
        places.of_query_block(i)
        n = places.listed(jnp.int32(0), range(2 * NH))
        places.padded(n)
        qs, dos = stacked(qdo_ref, i, 0), stacked(qdo_ref, i, 1)
        lse, delta = stat_ref[i, 0:1, :], stat_ref[i, 1:2, :]

        def step(at, number, dqt):
            blocks = places.blocks(at, number)
            keys = taken(kv_ref, blocks, KEYS)
            st = nt(keys, qs) * SCALE_LOG2 - lse
            p = jnp.exp2(jnp.where(places.mask(at, number), st, FILL))
            dp = nt(taken(kv_ref, blocks, VALUES), dos)
            return gradients(dqt, keys, p, dp, delta, qs, dos, acc_ref, blocks)

        wide = (n + 1) // STEP
        dqt = lax.fori_loop(0, wide, lambda c, t: step(STEP * c, STEP, t), dqt_ref[i])
        dqt = lax.fori_loop(
            wide, (n + STEP - 1) // STEP, lambda c, t: step(STEP * c, STEP // 2, t), dqt
        )
        for h in range(HEADS):
            cols = slice(h * B, (h + 1) * B)
            dq_ref[i, :, cols] = (dqt[:, cols] * SCALE).T.astype(BF)
        return carry

    lax.fori_loop(0, NH, one_block, 0)
    put_gradients(own_out, sib_out, acc_ref)


def near(facts, me, qdo, stat, own, sib, dqt):
    chunk = pl.BlockSpec((NH, B, 2 * D), lambda g: (0, 0, 0))
    return pl.pallas_call(
        near_kernel,
        grid=(1,),
        in_specs=[SM] * 2 + [VM] * 2 + [chunk] * 2 + [VM],
        out_specs=[VM] * 3,
        out_shape=[sds(NH, B, 2 * D)] * 2 + [sds(NH, B, W)],
        scratch_shapes=[
            pltpu.VMEM((2 * NH, B, 2 * D), BF),
            pltpu.VMEM((2 * NH, B, 2 * D), F32),
            pltpu.SMEM((2 * NH,), jnp.int32),
            pltpu.SMEM((2, 2 * NH + 8), jnp.int32),
        ],
        compiler_params=ROOM,
        cost_estimate=pl.CostEstimate(flops=7 * 10 ** 9, bytes_accessed=4 * 10 ** 6, transcendentals=0),
        name="near",
    )(facts, me, qdo, stat, own, sib, dqt)


def pack_kernel(me_ref, *refs):
    arrays, outs = refs[:-NH], refs[-NH:]
    for s, out in enumerate(outs):
        group, at = lax.rem(me_ref[2] + s, NH), 0
        for ref in arrays:
            width = ref.shape[1] // NH
            out[:, at:at + width] = ref[:, pl.ds(pl.multiple_of(group * width, width), width)]
            at += width


def pack(me, *arrays):
    width = sum(a.shape[1] for a in arrays) // NH
    return pl.pallas_call(
        pack_kernel,
        in_specs=[SM] + [VM] * len(arrays),
        out_specs=[VM] * NH,
        out_shape=[sds(B, width)] * NH,
        name="pack",
    )(me, *arrays)


def unpack_kernel(me_ref, *refs):
    early, late, outs = refs[:len(EARLY)], refs[len(EARLY):-4], refs[-4:]
    for s in range(NH):
        group = lax.rem(me_ref[2] + s, NH)
        wide = pl.ds(pl.multiple_of(group * W, W), W)
        narrow = pl.ds(pl.multiple_of(group * D, D), D)
        if s in EARLY:
            outs[0][:, wide] = early[EARLY.index(s)][...]
        else:
            outs[0][:, wide] = late[s][:, 2 * D + W:]
        outs[1][:, wide] = late[s][:, 2 * D:2 * D + W]
        outs[2][:, narrow] = late[s][:, KEYS]
        outs[3][:, narrow] = late[s][:, VALUES]


def unpack(me, early, late):
    return pl.pallas_call(
        unpack_kernel,
        in_specs=[SM] + [VM] * (len(EARLY) + NH),
        out_specs=[VM] * 4,
        out_shape=[sds(B, NH * W)] * 2 + [sds(B, NH * D)] * 2,
        name="unpack",
    )(me, *[early[s] for s in EARLY], *late)


def by_heads(piece, s, sign):
    perm = [
        ((c * NH + h) * NL + l, (l * NH + (h + sign * s) % NH) * NL + c)
        for c in range(2) for h in range(NH) for l in range(NL)
    ]
    return lax.ppermute(piece, ("core", HEAD_AXIS, "zl"), perm)


def to_seq(array, shift):
    return lax.ppermute(array, SEQ_AXIS, [(i, (i + shift) % NX) for i in range(NX)])


def to_sibling(array):
    return lax.ppermute(array, "core", [(0, 1), (1, 0)])


def on_device(queries, key_vectors, value_vectors, output_cotangent, doc_lengths, span_of):
    core, zl = lax.axis_index("core"), lax.axis_index("zl")
    me = jnp.stack([core, lax.axis_index(SEQ_AXIS), lax.axis_index(HEAD_AXIS)]).astype(jnp.int32)
    kv = pack(me, key_vectors, value_vectors)
    kv = jnp.stack([by_heads(kv[s], s, 1) for s in range(NH)])
    qdo = pack(me, queries, output_cotangent)
    qdo = jnp.stack([by_heads(qdo[s], s, 1) for s in range(NH)])
    facts = jnp.concatenate([span_of, doc_lengths])
    facts = jnp.where(core == zl, facts, to_sibling(facts))
    own = jnp.concatenate([kv] + [to_seq(kv, dx) for dx in range(1, NX)])
    own, qdo, facts = lax.optimization_barrier((own, qdo, facts))
    sib = to_sibling(own)
    o, stat, mine, theirs, dqt = far(facts, me, qdo, own, sib)

    def added(mine, theirs):
        return mine.astype(F32) + to_sibling(theirs).astype(F32)

    sums = added(mine, theirs).astype(BF)
    early = {s: by_heads(o[s], s, -1) for s in EARLY}
    dqt, sums = lax.optimization_barrier((dqt, sums))
    mine0, theirs0, dq = near(facts, me, qdo, stat, own, sib, dqt)
    came = [to_seq(sums[k * NH:(k + 1) * NH], -dx) for k, dx in enumerate(SHIFTS[:-1])]
    theirs0, came, early = lax.optimization_barrier((theirs0, came, early))
    total = added(mine0, theirs0)
    for part in came:
        total = total + part.astype(F32)
    total = total.astype(BF)
    late = [
        jnp.concatenate([total[s], dq[s]] + ([] if s in EARLY else [o[s]]), axis=1)
        for s in range(NH)
    ]
    late = [by_heads(late[s], s, -1) for s in range(NH)]
    return unpack(me, early, late)


def solution(mesh):
    split = Mesh(
        mesh.devices.reshape(-1, 2, NX, NH, NL), ("y", "core", "x", "zh", "zl")
    )
    rows = P(("y", "core", "x", "zh", "zl"), None)
    part = P(("y", "core"))
    return jax.shard_map(
        on_device,
        mesh=split,
        in_specs=(rows, rows, rows, rows, part, part),
        out_specs=(rows, rows, rows, rows),
        check_vma=False,
    )
```

```python
import jax
import jax.numpy as jnp
from jax import lax
from jax.experimental import pallas as pl
from jax.experimental.pallas import tpu as pltpu
from jax.sharding import Mesh, PartitionSpec as P

HEADS = 4
D = 128
B = 128
NX, NH, NL = 4, 4, 2
HEAD_AXIS, SEQ_AXIS = "zh", "x"
W = HEADS * B
SEEN = 18
STEP = 4
STEPS = (SEEN + 1 + STEP - 1) // STEP
SCALE = D ** -0.5
SCALE_LOG2 = SCALE * 1.4426950408889634
FILL = -1e30
BF, F32 = jnp.bfloat16, jnp.float32
VM = pl.BlockSpec(memory_space=pltpu.VMEM)
SM = pl.BlockSpec(memory_space=pltpu.SMEM)
HBM = pl.BlockSpec(memory_space=pl.ANY)
ROOM = pltpu.CompilerParams(vmem_limit_bytes=48 * 2 ** 20)


def nt(a, b):
    return lax.dot_general(a, b, (((1,), (1,)), ((), ())), preferred_element_type=F32)


def tn(a, b):
    return lax.dot_general(a, b, (((0,), (0,)), ((), ())), preferred_element_type=F32)


def nn(a, b):
    return lax.dot_general(a, b, (((1,), (0,)), ((), ())), preferred_element_type=F32)


def sds(*shape, dtype=BF):
    return jax.ShapeDtypeStruct(shape, dtype)


class Places:
    def __init__(self, fact_ref, me_ref, shifts, table_ref, list_ref):
        self.fact_ref, self.me_ref = fact_ref, me_ref
        self.table_ref, self.list_ref = table_ref, list_ref
        self.count = 2 * NH * len(shifts)
        self.ends = []
        total = jnp.int32(0)
        for i in range(4):
            total = total + fact_ref[NX * NH * NL + i]
            self.ends.append(total)
        for k, dx in enumerate(shifts):
            for side in range(2):
                for step in range(NH):
                    table_ref[(k * 2 + side) * NH + step] = self.span(dx, step, side)

    def span(self, dx, step, side):
        e, seq, head = self.me_ref[0], self.me_ref[1], self.me_ref[2]
        from_x = lax.rem(seq + NX - dx, NX)
        from_zh = lax.rem(head + NH - step, NH)
        return self.fact_ref[(from_x * NH + from_zh) * NL + lax.rem(e + side, NL)]

    def of_query_block(self, i):
        span = self.span(0, i, 0)
        first = span * B
        self.q_pos = first + lax.rem(lax.broadcasted_iota(jnp.int32, (1, W), 1), B)
        self.q_start = jnp.zeros((1, W), jnp.int32)
        start_first = jnp.int32(0)
        for e in self.ends:
            start_first = jnp.where(e <= first, e, start_first)
            self.q_start = jnp.where(e <= self.q_pos, e, self.q_start)
        self.low, self.high = start_first // B, span

    def listed(self, n, entries):
        for j in entries:
            s = self.table_ref[j]
            self.list_ref[0, n] = j
            self.list_ref[1, n] = s * B
            n = n + jnp.where((s >= self.low) & (s <= self.high), 1, 0)
        return n

    def padded(self, n):
        for j in range(STEP):
            self.list_ref[0, n + j] = 0
            self.list_ref[1, n + j] = SEEN * B * 4

    def blocks(self, at, number):
        return [self.list_ref[0, at + j] for j in range(number)]

    def mask(self, at, number):
        row = lax.broadcasted_iota(jnp.int32, (B, W), 0)
        parts = []
        for j in range(number):
            k_pos = row + self.list_ref[1, at + j]
            parts.append((k_pos >= self.q_start) & (k_pos <= self.q_pos))
        return jnp.concatenate(parts, axis=0)


def stacked(ref, i, which):
    return jnp.concatenate(
        [ref[i, :, (which * HEADS + h) * D:(which * HEADS + h + 1) * D] for h in range(HEADS)], axis=0
    )


def taken(ref, blocks, cols):
    return jnp.concatenate([ref[block, :, cols] for block in blocks], axis=0)


SHIFTS = (1, 2, 3, 0)
EARLY = (1,)
FAR = 2 * NH * (NX - 1)
KEYS, VALUES = slice(0, D), slice(D, 2 * D)


def gradients(dqt, keys, p, dp, delta, qs, dos, acc_ref, blocks):
    ds = (p * (dp - delta)).astype(BF)
    dv = nn(p.astype(BF), dos)
    dk = nn(ds, qs)
    for j, block in enumerate(blocks):
        acc_ref[block, :, KEYS] += dk[j * B:(j + 1) * B]
        acc_ref[block, :, VALUES] += dv[j * B:(j + 1) * B]
    return dqt + tn(keys, ds)


def put_gradients(own_out, sib_out, acc_ref):
    for ref, side in ((own_out, 0), (sib_out, 1)):
        for j in range(ref.shape[0]):
            at = (j // NH * 2 + side) * NH + j % NH
            ref[j, :, KEYS] = (acc_ref[at, :, KEYS] * SCALE).astype(BF)
            ref[j, :, VALUES] = acc_ref[at, :, VALUES].astype(BF)


def far_kernel(fact_ref, me_ref, qdo_ref, own_ref, sib_ref,
               o_ref, stat_ref, own_out, sib_out, dqt_out,
               s_ref, kv_ref, acc_ref, table_ref, list_ref, sems, sum_ref):
    copies = [
        pltpu.make_async_copy(
            ref.at[dx * NH:(dx + 1) * NH],
            kv_ref.at[(2 * k + side) * NH:(2 * k + side + 1) * NH],
            sems.at[2 * k + side],
        )
        for k, dx in enumerate(SHIFTS) for side, ref in enumerate((own_ref, sib_ref))
    ]
    for copy in copies:
        copy.start()
    places = Places(fact_ref, me_ref, SHIFTS, table_ref, list_ref)
    acc_ref[...] = jnp.zeros_like(acc_ref)
    for copy in copies:
        copy.wait()

    def one_block(i, carry):
        places.of_query_block(i)
        far = places.listed(jnp.int32(0), range(FAR))
        list_ref[0, far] = 0
        list_ref[1, far] = SEEN * B * 4
        far = (far + 1) // 2 * 2
        n = places.listed(far, range(FAR, 2 * NX * NH))
        places.padded(n)
        steps = (n + STEP - 1) // STEP
        qs, dos = stacked(qdo_ref, i, 0), stacked(qdo_ref, i, 1)

        def score_step(c, m):
            blocks = places.blocks(STEP * c, STEP)
            st = nt(taken(kv_ref, blocks, KEYS), qs) * SCALE_LOG2
            st = jnp.where(places.mask(STEP * c, STEP), st, FILL)
            s_ref[c] = st
            return jnp.maximum(m, jnp.max(st.reshape(-1, 8, W), axis=0))

        m = lax.fori_loop(0, steps, score_step, jnp.full((8, W), FILL, F32))
        m = jnp.max(m, axis=0, keepdims=True)

        def weigh_step(c, state):
            l, ot = state
            blocks = places.blocks(STEP * c, STEP)
            p = jnp.exp2(s_ref[c] - m)
            return (
                l + jnp.sum(p.reshape(-1, 8, W), axis=0),
                ot + tn(taken(kv_ref, blocks, VALUES), p.astype(BF)),
            )

        state = jnp.zeros((8, W), F32), jnp.zeros((D, W), F32)
        l, ot = lax.fori_loop(0, steps, weigh_step, state)
        l = jnp.sum(l, axis=0, keepdims=True)
        ob = (ot * (1.0 / l)).astype(BF)
        delta = []
        for h in range(HEADS):
            cols = slice(h * B, (h + 1) * B)
            of = ob[:, cols].astype(F32)
            o_ref[i, :, cols] = of.T.astype(BF)
            dot = qdo_ref[i, :, W + h * B:W + (h + 1) * B].astype(F32).T
            delta.append(jnp.sum(of * dot, axis=0, keepdims=True))
        delta = jnp.concatenate(delta, axis=1)
        lse = m + jnp.log2(l)
        stat_ref[i, 0:1, :] = lse
        stat_ref[i, 1:2, :] = delta

        def back_step(c, part, number, dqt):
            at = STEP * c + part
            blocks = places.blocks(at, number)
            p = jnp.exp2(s_ref[c, part * B:(part + number) * B] - lse)
            dp = nt(taken(kv_ref, blocks, VALUES), dos)
            keys = taken(kv_ref, blocks, KEYS)
            return gradients(dqt, keys, p, dp, delta, qs, dos, acc_ref, blocks)

        wide = far // STEP
        dqt = lax.fori_loop(
            0, wide, lambda c, t: back_step(c, 0, STEP, t), jnp.zeros((D, W), F32)
        )
        sum_ref[i] = lax.fori_loop(
            wide, (far + STEP - 1) // STEP, lambda c, t: back_step(c, 0, STEP // 2, t), dqt
        )
        return carry

    lax.fori_loop(0, NH, one_block, 0)
    copy = pltpu.make_async_copy(sum_ref, dqt_out, sems.at[2 * NX])
    copy.start()
    put_gradients(own_out, sib_out, acc_ref)
    copy.wait()


def far(facts, me, qdo, own, sib):
    blocks = 2 * NX * NH
    return pl.pallas_call(
        far_kernel,
        in_specs=[SM] * 2 + [VM] + [HBM] * 2,
        out_specs=[VM] * 4 + [HBM],
        out_shape=[sds(NH, B, W), sds(NH, 8, W, dtype=F32)]
        + [sds(FAR // 2, B, 2 * D)] * 2 + [sds(NH, D, W, dtype=F32)],
        scratch_shapes=[
            pltpu.VMEM((STEPS, STEP * B, W), F32),
            pltpu.VMEM((blocks, B, 2 * D), BF),
            pltpu.VMEM((FAR, B, 2 * D), F32),
            pltpu.SMEM((blocks,), jnp.int32),
            pltpu.SMEM((2, blocks + 8), jnp.int32),
            pltpu.SemaphoreType.DMA((2 * NX + 1,)),
            pltpu.VMEM((NH, D, W), F32),
        ],
        compiler_params=ROOM,
        cost_estimate=pl.CostEstimate(flops=20 * 10 ** 9, bytes_accessed=4 * 10 ** 6, transcendentals=0),
        name="far",
    )(facts, me, qdo, own, sib)


def near_kernel(fact_ref, me_ref, qdo_ref, stat_ref, own_ref, sib_ref, dqt_ref,
                own_out, sib_out, dq_ref, kv_ref, acc_ref, table_ref, list_ref, sem, sum_ref):
    copy = pltpu.make_async_copy(dqt_ref, sum_ref, sem.at[0])
    copy.start()
    kv_ref[:NH] = own_ref[...]
    kv_ref[NH:] = sib_ref[...]
    places = Places(fact_ref, me_ref, (0,), table_ref, list_ref)
    acc_ref[...] = jnp.zeros_like(acc_ref)
    copy.wait()

    def one_block(i, carry):
        places.of_query_block(i)
        n = places.listed(jnp.int32(0), range(2 * NH))
        places.padded(n)
        qs, dos = stacked(qdo_ref, i, 0), stacked(qdo_ref, i, 1)
        lse, delta = stat_ref[i, 0:1, :], stat_ref[i, 1:2, :]

        def step(at, number, dqt):
            blocks = places.blocks(at, number)
            keys = taken(kv_ref, blocks, KEYS)
            st = nt(keys, qs) * SCALE_LOG2 - lse
            p = jnp.exp2(jnp.where(places.mask(at, number), st, FILL))
            dp = nt(taken(kv_ref, blocks, VALUES), dos)
            return gradients(dqt, keys, p, dp, delta, qs, dos, acc_ref, blocks)

        wide = (n + 1) // STEP
        dqt = lax.fori_loop(0, wide, lambda c, t: step(STEP * c, STEP, t), sum_ref[i])
        dqt = lax.fori_loop(
            wide, (n + STEP - 1) // STEP, lambda c, t: step(STEP * c, STEP // 2, t), dqt
        )
        for h in range(HEADS):
            cols = slice(h * B, (h + 1) * B)
            dq_ref[i, :, cols] = (dqt[:, cols] * SCALE).T.astype(BF)
        return carry

    lax.fori_loop(0, NH, one_block, 0)
    put_gradients(own_out, sib_out, acc_ref)


def near(facts, me, qdo, stat, own, sib, dqt):
    chunk = pl.BlockSpec((NH, B, 2 * D), lambda g: (0, 0, 0))
    return pl.pallas_call(
        near_kernel,
        grid=(1,),
        in_specs=[SM] * 2 + [VM] * 2 + [chunk] * 2 + [HBM],
        out_specs=[VM] * 3,
        out_shape=[sds(NH, B, 2 * D)] * 2 + [sds(NH, B, W)],
        scratch_shapes=[
            pltpu.VMEM((2 * NH, B, 2 * D), BF),
            pltpu.VMEM((2 * NH, B, 2 * D), F32),
            pltpu.SMEM((2 * NH,), jnp.int32),
            pltpu.SMEM((2, 2 * NH + 8), jnp.int32),
            pltpu.SemaphoreType.DMA((1,)),
            pltpu.VMEM((NH, D, W), F32),
        ],
        compiler_params=ROOM,
        cost_estimate=pl.CostEstimate(flops=7 * 10 ** 9, bytes_accessed=4 * 10 ** 6, transcendentals=0),
        name="near",
    )(facts, me, qdo, stat, own, sib, dqt)


def pack_kernel(*refs):
    arrays, outs = refs[:-NH], refs[-NH:]
    for s, out in enumerate(outs):
        group, at = lax.rem(lax.axis_index(HEAD_AXIS).astype(jnp.int32) + s, NH), 0
        for ref in arrays:
            width = ref.shape[1] // NH
            out[:, at:at + width] = ref[:, pl.ds(pl.multiple_of(group * width, width), width)]
            at += width


def pack(*arrays):
    width = sum(a.shape[1] for a in arrays) // NH
    return pl.pallas_call(
        pack_kernel,
        in_specs=[VM] * len(arrays),
        out_specs=[VM] * NH,
        out_shape=[sds(B, width)] * NH,
        name="pack",
    )(*arrays)


def unpack_kernel(me_ref, *refs):
    early, late, outs = refs[:len(EARLY)], refs[len(EARLY):-4], refs[-4:]
    for s in range(NH):
        group = lax.rem(me_ref[2] + s, NH)
        wide = pl.ds(pl.multiple_of(group * W, W), W)
        narrow = pl.ds(pl.multiple_of(group * D, D), D)
        if s in EARLY:
            outs[0][:, wide] = early[EARLY.index(s)][...]
        else:
            outs[0][:, wide] = late[s][:, 2 * D + W:]
        outs[1][:, wide] = late[s][:, 2 * D:2 * D + W]
        outs[2][:, narrow] = late[s][:, KEYS]
        outs[3][:, narrow] = late[s][:, VALUES]


def unpack(me, early, late):
    return pl.pallas_call(
        unpack_kernel,
        in_specs=[SM] + [VM] * (len(EARLY) + NH),
        out_specs=[VM] * 4,
        out_shape=[sds(B, NH * W)] * 2 + [sds(B, NH * D)] * 2,
        name="unpack",
    )(me, *[early[s] for s in EARLY], *late)


def by_heads(piece, s, sign):
    perm = [
        ((c * NH + h) * NL + l, (l * NH + (h + sign * s) % NH) * NL + c)
        for c in range(2) for h in range(NH) for l in range(NL)
    ]
    return lax.ppermute(piece, ("core", HEAD_AXIS, "zl"), perm)


def to_seq(array, shift):
    return lax.ppermute(array, SEQ_AXIS, [(i, (i + shift) % NX) for i in range(NX)])


def to_sibling(array):
    return lax.ppermute(array, "core", [(0, 1), (1, 0)])


def on_device(queries, key_vectors, value_vectors, output_cotangent, doc_lengths, span_of):
    core, zl = lax.axis_index("core"), lax.axis_index("zl")
    me = jnp.stack([core, lax.axis_index(SEQ_AXIS), lax.axis_index(HEAD_AXIS)]).astype(jnp.int32)
    kv = pack(key_vectors, value_vectors)
    kv = jnp.stack([by_heads(kv[s], s, 1) for s in range(NH)])
    qdo = pack(queries, output_cotangent)
    qdo = jnp.stack([by_heads(qdo[s], s, 1) for s in range(NH)])
    facts = jnp.concatenate([span_of, doc_lengths])
    facts = jnp.where(core == zl, facts, to_sibling(facts))
    own = jnp.concatenate([kv] + [to_seq(kv, dx) for dx in range(1, NX)])
    own, qdo, facts = lax.optimization_barrier((own, qdo, facts))
    sib = to_sibling(own)
    o, stat, mine, theirs, dqt = far(facts, me, qdo, own, sib)

    def added(mine, theirs):
        return mine.astype(F32) + to_sibling(theirs).astype(F32)

    sums = added(mine, theirs).astype(BF)
    early = {s: by_heads(o[s], s, -1) for s in EARLY}
    dqt, sums = lax.optimization_barrier((dqt, sums))
    mine0, theirs0, dq = near(facts, me, qdo, stat, own, sib, dqt)
    came = [to_seq(sums[k * NH:(k + 1) * NH], -dx) for k, dx in enumerate(SHIFTS[:-1])]
    theirs0, came, early = lax.optimization_barrier((theirs0, came, early))
    total = added(mine0, theirs0)
    for part in came:
        total = total + part.astype(F32)
    total = total.astype(BF)
    late = [
        jnp.concatenate([total[s], dq[s]] + ([] if s in EARLY else [o[s]]), axis=1)
        for s in range(NH)
    ]
    late = [by_heads(late[s], s, -1) for s in range(NH)]
    return unpack(me, early, late)


def solution(mesh):
    split = Mesh(
        mesh.devices.reshape(-1, 2, NX, NH, NL), ("y", "core", "x", "zh", "zl")
    )
    rows = P(("y", "core", "x", "zh", "zl"), None)
    part = P(("y", "core"))
    return jax.shard_map(
        on_device,
        mesh=split,
        in_specs=(rows, rows, rows, rows, part, part),
        out_specs=(rows, rows, rows, rows),
        check_vma=False,
    )
```

```python
import jax
import jax.numpy as jnp
from jax import lax
from jax.experimental import pallas as pl
from jax.experimental.pallas import tpu as pltpu
from jax.sharding import Mesh, PartitionSpec as P

HEADS = 4
D = 128
B = 128
NX, NH, NL = 4, 4, 2
HEAD_AXIS, SEQ_AXIS = "zh", "x"
W = HEADS * B
SEEN = 18
STEP = 4
STEPS = (SEEN + 1 + STEP - 1) // STEP
SCALE = D ** -0.5
SCALE_LOG2 = SCALE * 1.4426950408889634
FILL = -1e30
BF, F32 = jnp.bfloat16, jnp.float32
VM = pl.BlockSpec(memory_space=pltpu.VMEM)
SM = pl.BlockSpec(memory_space=pltpu.SMEM)
HBM = pl.BlockSpec(memory_space=pl.ANY)
ROOM = pltpu.CompilerParams(vmem_limit_bytes=48 * 2 ** 20)


def nt(a, b):
    return lax.dot_general(a, b, (((1,), (1,)), ((), ())), preferred_element_type=F32)


def tn(a, b):
    return lax.dot_general(a, b, (((0,), (0,)), ((), ())), preferred_element_type=F32)


def nn(a, b):
    return lax.dot_general(a, b, (((1,), (0,)), ((), ())), preferred_element_type=F32)


def sds(*shape, dtype=BF):
    return jax.ShapeDtypeStruct(shape, dtype)


class Places:
    def __init__(self, fact_ref, me_ref, shifts, table_ref, list_ref):
        self.fact_ref, self.me_ref = fact_ref, me_ref
        self.table_ref, self.list_ref = table_ref, list_ref
        self.count = 2 * NH * len(shifts)
        self.ends = []
        total = jnp.int32(0)
        for i in range(4):
            total = total + fact_ref[NX * NH * NL + i]
            self.ends.append(total)
        for k, dx in enumerate(shifts):
            for side in range(2):
                for step in range(NH):
                    table_ref[(k * 2 + side) * NH + step] = self.span(dx, step, side)

    def span(self, dx, step, side):
        e, seq, head = self.me_ref[0], self.me_ref[1], self.me_ref[2]
        from_x = lax.rem(seq + NX - dx, NX)
        from_zh = lax.rem(head + NH - step, NH)
        return self.fact_ref[(from_x * NH + from_zh) * NL + lax.rem(e + side, NL)]

    def of_query_block(self, i):
        span = self.span(0, i, 0)
        first = span * B
        self.q_pos = first + lax.rem(lax.broadcasted_iota(jnp.int32, (1, W), 1), B)
        self.q_start = jnp.zeros((1, W), jnp.int32)
        start_first = jnp.int32(0)
        for e in self.ends:
            start_first = jnp.where(e <= first, e, start_first)
            self.q_start = jnp.where(e <= self.q_pos, e, self.q_start)
        self.low, self.high = start_first // B, span

    def listed(self, n, entries):
        for j in entries:
            s = self.table_ref[j]
            self.list_ref[0, n] = j
            self.list_ref[1, n] = s * B
            n = n + jnp.where((s >= self.low) & (s <= self.high), 1, 0)
        return n

    def padded(self, n):
        for j in range(STEP):
            self.list_ref[0, n + j] = 0
            self.list_ref[1, n + j] = SEEN * B * 4

    def blocks(self, at, number):
        return [self.list_ref[0, at + j] for j in range(number)]

    def mask(self, at, number):
        row = lax.broadcasted_iota(jnp.int32, (B, W), 0)
        parts = []
        for j in range(number):
            k_pos = row + self.list_ref[1, at + j]
            parts.append((k_pos >= self.q_start) & (k_pos <= self.q_pos))
        return jnp.concatenate(parts, axis=0)


def stacked(ref, i, which):
    return jnp.concatenate(
        [ref[i, :, (which * HEADS + h) * D:(which * HEADS + h + 1) * D] for h in range(HEADS)], axis=0
    )


def taken(ref, blocks, cols):
    return jnp.concatenate([ref[block, :, cols] for block in blocks], axis=0)


SHIFTS = (1, 2, 3, 0)
EARLY = (2,)
FAR = 2 * NH * (NX - 1)
KEYS, VALUES = slice(0, D), slice(D, 2 * D)


def gradients(dqt, keys, p, dp, delta, qs, dos, acc_ref, blocks):
    ds = (p * (dp - delta)).astype(BF)
    dv = nn(p.astype(BF), dos)
    dk = nn(ds, qs)
    for j, block in enumerate(blocks):
        acc_ref[block, :, KEYS] += dk[j * B:(j + 1) * B]
        acc_ref[block, :, VALUES] += dv[j * B:(j + 1) * B]
    return dqt + tn(keys, ds)


def put_gradients(own_out, sib_out, acc_ref):
    for ref, side in ((own_out, 0), (sib_out, 1)):
        for j in range(ref.shape[0]):
            at = (j // NH * 2 + side) * NH + j % NH
            ref[j, :, KEYS] = (acc_ref[at, :, KEYS] * SCALE).astype(BF)
            ref[j, :, VALUES] = acc_ref[at, :, VALUES].astype(BF)


def far_kernel(fact_ref, me_ref, qdo_ref, own_ref, sib_ref,
               o_ref, stat_ref, own_out, sib_out, dqt_out,
               s_ref, kv_ref, acc_ref, table_ref, list_ref, sems, sum_ref):
    copies = [
        pltpu.make_async_copy(
            ref.at[dx * NH:(dx + 1) * NH],
            kv_ref.at[(2 * k + side) * NH:(2 * k + side + 1) * NH],
            sems.at[2 * k + side],
        )
        for k, dx in enumerate(SHIFTS) for side, ref in enumerate((own_ref, sib_ref))
    ]
    for copy in copies:
        copy.start()
    places = Places(fact_ref, me_ref, SHIFTS, table_ref, list_ref)
    acc_ref[...] = jnp.zeros_like(acc_ref)
    for copy in copies:
        copy.wait()

    def one_block(i, carry):
        places.of_query_block(i)
        far = places.listed(jnp.int32(0), range(FAR))
        list_ref[0, far] = 0
        list_ref[1, far] = SEEN * B * 4
        far = (far + 1) // 2 * 2
        n = places.listed(far, range(FAR, 2 * NX * NH))
        places.padded(n)
        steps = (n + STEP - 1) // STEP
        qs, dos = stacked(qdo_ref, i, 0), stacked(qdo_ref, i, 1)

        def score_step(c, m):
            blocks = places.blocks(STEP * c, STEP)
            st = nt(taken(kv_ref, blocks, KEYS), qs) * SCALE_LOG2
            st = jnp.where(places.mask(STEP * c, STEP), st, FILL)
            s_ref[c] = st
            return jnp.maximum(m, jnp.max(st.reshape(-1, 8, W), axis=0))

        m = lax.fori_loop(0, steps, score_step, jnp.full((8, W), FILL, F32))
        m = jnp.max(m, axis=0, keepdims=True)

        def weigh_step(c, state):
            l, ot = state
            blocks = places.blocks(STEP * c, STEP)
            p = jnp.exp2(s_ref[c] - m)
            return (
                l + jnp.sum(p.reshape(-1, 8, W), axis=0),
                ot + tn(taken(kv_ref, blocks, VALUES), p.astype(BF)),
            )

        state = jnp.zeros((8, W), F32), jnp.zeros((D, W), F32)
        l, ot = lax.fori_loop(0, steps, weigh_step, state)
        l = jnp.sum(l, axis=0, keepdims=True)
        ob = (ot * (1.0 / l)).astype(BF)
        delta = []
        for h in range(HEADS):
            cols = slice(h * B, (h + 1) * B)
            of = ob[:, cols].astype(F32)
            o_ref[i, :, cols] = of.T.astype(BF)
            dot = qdo_ref[i, :, W + h * B:W + (h + 1) * B].astype(F32).T
            delta.append(jnp.sum(of * dot, axis=0, keepdims=True))
        delta = jnp.concatenate(delta, axis=1)
        lse = m + jnp.log2(l)
        stat_ref[i, 0:1, :] = lse
        stat_ref[i, 1:2, :] = delta

        def back_step(c, part, number, dqt):
            at = STEP * c + part
            blocks = places.blocks(at, number)
            p = jnp.exp2(s_ref[c, part * B:(part + number) * B] - lse)
            dp = nt(taken(kv_ref, blocks, VALUES), dos)
            keys = taken(kv_ref, blocks, KEYS)
            return gradients(dqt, keys, p, dp, delta, qs, dos, acc_ref, blocks)

        wide = far // STEP
        dqt = lax.fori_loop(
            0, wide, lambda c, t: back_step(c, 0, STEP, t), jnp.zeros((D, W), F32)
        )
        sum_ref[i] = lax.fori_loop(
            wide, (far + STEP - 1) // STEP, lambda c, t: back_step(c, 0, STEP // 2, t), dqt
        )
        return carry

    lax.fori_loop(0, NH, one_block, 0)
    copy = pltpu.make_async_copy(sum_ref, dqt_out, sems.at[2 * NX])
    copy.start()
    put_gradients(own_out, sib_out, acc_ref)
    copy.wait()


def far(facts, me, qdo, own, sib):
    blocks = 2 * NX * NH
    return pl.pallas_call(
        far_kernel,
        in_specs=[SM] * 2 + [VM] + [HBM] * 2,
        out_specs=[VM] * 4 + [HBM],
        out_shape=[sds(NH, B, W), sds(NH, 8, W, dtype=F32)]
        + [sds(FAR // 2, B, 2 * D)] * 2 + [sds(NH, D, W, dtype=F32)],
        scratch_shapes=[
            pltpu.VMEM((STEPS, STEP * B, W), F32),
            pltpu.VMEM((blocks, B, 2 * D), BF),
            pltpu.VMEM((FAR, B, 2 * D), F32),
            pltpu.SMEM((blocks,), jnp.int32),
            pltpu.SMEM((2, blocks + 8), jnp.int32),
            pltpu.SemaphoreType.DMA((2 * NX + 1,)),
            pltpu.VMEM((NH, D, W), F32),
        ],
        compiler_params=ROOM,
        cost_estimate=pl.CostEstimate(flops=20 * 10 ** 9, bytes_accessed=4 * 10 ** 6, transcendentals=0),
        name="far",
    )(facts, me, qdo, own, sib)


def near_kernel(fact_ref, me_ref, qdo_ref, stat_ref, own_ref, sib_ref, dqt_ref,
                own_out, sib_out, dq_ref, kv_ref, acc_ref, table_ref, list_ref, sem, sum_ref):
    copy = pltpu.make_async_copy(dqt_ref, sum_ref, sem.at[0])
    copy.start()
    kv_ref[:NH] = own_ref[...]
    kv_ref[NH:] = sib_ref[...]
    places = Places(fact_ref, me_ref, (0,), table_ref, list_ref)
    acc_ref[...] = jnp.zeros_like(acc_ref)
    copy.wait()

    def one_block(i, carry):
        places.of_query_block(i)
        n = places.listed(jnp.int32(0), range(2 * NH))
        places.padded(n)
        qs, dos = stacked(qdo_ref, i, 0), stacked(qdo_ref, i, 1)
        lse, delta = stat_ref[i, 0:1, :], stat_ref[i, 1:2, :]

        def step(at, number, dqt):
            blocks = places.blocks(at, number)
            keys = taken(kv_ref, blocks, KEYS)
            st = nt(keys, qs) * SCALE_LOG2 - lse
            p = jnp.exp2(jnp.where(places.mask(at, number), st, FILL))
            dp = nt(taken(kv_ref, blocks, VALUES), dos)
            return gradients(dqt, keys, p, dp, delta, qs, dos, acc_ref, blocks)

        wide = (n + 1) // STEP
        dqt = lax.fori_loop(0, wide, lambda c, t: step(STEP * c, STEP, t), sum_ref[i])
        dqt = lax.fori_loop(
            wide, (n + STEP - 1) // STEP, lambda c, t: step(STEP * c, STEP // 2, t), dqt
        )
        for h in range(HEADS):
            cols = slice(h * B, (h + 1) * B)
            dq_ref[i, :, cols] = (dqt[:, cols] * SCALE).T.astype(BF)
        return carry

    lax.fori_loop(0, NH, one_block, 0)
    put_gradients(own_out, sib_out, acc_ref)


def near(facts, me, qdo, stat, own, sib, dqt):
    chunk = pl.BlockSpec((NH, B, 2 * D), lambda g: (0, 0, 0))
    return pl.pallas_call(
        near_kernel,
        grid=(1,),
        in_specs=[SM] * 2 + [VM] * 2 + [chunk] * 2 + [HBM],
        out_specs=[VM] * 3,
        out_shape=[sds(NH, B, 2 * D)] * 2 + [sds(NH, B, W)],
        scratch_shapes=[
            pltpu.VMEM((2 * NH, B, 2 * D), BF),
            pltpu.VMEM((2 * NH, B, 2 * D), F32),
            pltpu.SMEM((2 * NH,), jnp.int32),
            pltpu.SMEM((2, 2 * NH + 8), jnp.int32),
            pltpu.SemaphoreType.DMA((1,)),
            pltpu.VMEM((NH, D, W), F32),
        ],
        compiler_params=ROOM,
        cost_estimate=pl.CostEstimate(flops=7 * 10 ** 9, bytes_accessed=4 * 10 ** 6, transcendentals=0),
        name="near",
    )(facts, me, qdo, stat, own, sib, dqt)


def pack_kernel(*refs):
    arrays, outs = refs[:-NH], refs[-NH:]
    for s, out in enumerate(outs):
        group, at = lax.rem(lax.axis_index(HEAD_AXIS).astype(jnp.int32) + s, NH), 0
        for ref in arrays:
            width = ref.shape[1] // NH
            out[:, at:at + width] = ref[:, pl.ds(pl.multiple_of(group * width, width), width)]
            at += width


def pack(*arrays):
    width = sum(a.shape[1] for a in arrays) // NH
    return pl.pallas_call(
        pack_kernel,
        in_specs=[VM] * len(arrays),
        out_specs=[VM] * NH,
        out_shape=[sds(B, width)] * NH,
        name="pack",
    )(*arrays)


def unpack_kernel(me_ref, *refs):
    early, late, outs = refs[:len(EARLY)], refs[len(EARLY):-4], refs[-4:]
    for s in range(NH):
        group = lax.rem(me_ref[2] + s, NH)
        wide = pl.ds(pl.multiple_of(group * W, W), W)
        narrow = pl.ds(pl.multiple_of(group * D, D), D)
        if s in EARLY:
            outs[0][:, wide] = early[EARLY.index(s)][...]
        else:
            outs[0][:, wide] = late[s][:, 2 * D + W:]
        outs[1][:, wide] = late[s][:, 2 * D:2 * D + W]
        outs[2][:, narrow] = late[s][:, KEYS]
        outs[3][:, narrow] = late[s][:, VALUES]


def unpack(me, early, late):
    return pl.pallas_call(
        unpack_kernel,
        in_specs=[SM] + [VM] * (len(EARLY) + NH),
        out_specs=[VM] * 4,
        out_shape=[sds(B, NH * W)] * 2 + [sds(B, NH * D)] * 2,
        name="unpack",
    )(me, *[early[s] for s in EARLY], *late)


def by_heads(piece, s, sign):
    perm = [
        ((c * NH + h) * NL + l, (l * NH + (h + sign * s) % NH) * NL + c)
        for c in range(2) for h in range(NH) for l in range(NL)
    ]
    return lax.ppermute(piece, ("core", HEAD_AXIS, "zl"), perm)


def to_seq(array, shift):
    return lax.ppermute(array, SEQ_AXIS, [(i, (i + shift) % NX) for i in range(NX)])


def to_sibling(array):
    return lax.ppermute(array, "core", [(0, 1), (1, 0)])


def on_device(queries, key_vectors, value_vectors, output_cotangent, doc_lengths, span_of):
    core, zl = lax.axis_index("core"), lax.axis_index("zl")
    me = jnp.stack([core, lax.axis_index(SEQ_AXIS), lax.axis_index(HEAD_AXIS)]).astype(jnp.int32)
    kv = pack(key_vectors, value_vectors)
    kv = jnp.stack([by_heads(kv[s], s, 1) for s in range(NH)])
    qdo = pack(queries, output_cotangent)
    qdo = jnp.stack([by_heads(qdo[s], s, 1) for s in range(NH)])
    facts = jnp.concatenate([span_of, doc_lengths])
    facts = jnp.where(core == zl, facts, to_sibling(facts))
    own = jnp.concatenate([kv] + [to_seq(kv, dx) for dx in range(1, NX)])
    own, qdo, facts = lax.optimization_barrier((own, qdo, facts))
    sib = to_sibling(own)
    o, stat, mine, theirs, dqt = far(facts, me, qdo, own, sib)

    def added(mine, theirs):
        return mine.astype(F32) + to_sibling(theirs).astype(F32)

    sums = added(mine, theirs).astype(BF)
    early = {s: by_heads(o[s], s, -1) for s in EARLY}
    dqt, sums = lax.optimization_barrier((dqt, sums))
    mine0, theirs0, dq = near(facts, me, qdo, stat, own, sib, dqt)
    came = [to_seq(sums[k * NH:(k + 1) * NH], -dx) for k, dx in enumerate(SHIFTS[:-1])]
    theirs0, came, early = lax.optimization_barrier((theirs0, came, early))
    total = added(mine0, theirs0)
    for part in came:
        total = total + part.astype(F32)
    total = total.astype(BF)
    late = [
        jnp.concatenate([total[s], dq[s]] + ([] if s in EARLY else [o[s]]), axis=1)
        for s in range(NH)
    ]
    late = [by_heads(late[s], s, -1) for s in range(NH)]
    return unpack(me, early, late)


def solution(mesh):
    split = Mesh(
        mesh.devices.reshape(-1, 2, NX, NH, NL), ("y", "core", "x", "zh", "zl")
    )
    rows = P(("y", "core", "x", "zh", "zl"), None)
    part = P(("y", "core"))
    return jax.shard_map(
        on_device,
        mesh=split,
        in_specs=(rows, rows, rows, rows, part, part),
        out_specs=(rows, rows, rows, rows),
        check_vma=False,
    )
```
